128 devices in a mesh: ctx: 16 (over x, y_hi, core), tp: 8 (over y_lo, z).
Axes of the slice: x: 4, y: 4 (y_hi: 2, y_lo: 2; y = y_hi * 2 + y_lo), z: 4, core: 2. Of those that a mesh axis runs over, the one named last changes fastest.
Arguments:
- queries: bfloat16 [2048, 16384], P('ctx', 'tp'), may hold values from -48 to 48
- cache_keys: bfloat16 [16384, 1024], P('ctx', 'tp'), may hold values from -6.4 to 6.4
- cache_values: bfloat16 [16384, 1024], P('ctx', 'tp'), may hold values from -6 to 6
- new_keys: bfloat16 [2048, 1024], P(('ctx', 'tp')), may hold values from -6.375 to 6.375
- new_values: bfloat16 [2048, 1024], P(('ctx', 'tp')), may hold values from -6 to 6
- sources: int32 [2048], replicated, may hold values from 0 to 2047, each once
Outputs:
- attended: bfloat16 [2048, 16384], P('ctx', 'tp')
The draws below stay inside these ranges and needn't reach their ends.
Inputs may be any that keep to these rules, and one draw needn't show every extreme that they name: `sources`: every new token appears once; append slot s belongs to owner s // 128.
All inputs are finite; a program needn't handle non-finite values.
Results may differ from the reference program's by a relative error of at most 0.0015.
The reference program's roundings to bfloat16 on the way count: a program that leaves them out, or rounds other values in their place, can miss the bound.
Values may be sent and summed in bfloat16 or wider, within the bound.
A program may use at most 128 MiB of HBM per device.

```python
import jax
import jax.numpy as jnp
from jax import lax

HEADS = 128
KV_HEADS = 8
HEAD_DIM = 128
NEW_DEV = 128
CACHE_DEV = 1024
NEW_TOKENS = 2048
CTX = 16384


def shared_keys(key):
    base = jax.random.normal(jax.random.fold_in(key, 100), (CTX, KV_HEADS * HEAD_DIM), jnp.float32)
    base = jnp.clip(1.6 * base, -6.375, 6.375)
    count = NEW_TOKENS // 64
    index = jnp.arange(count)
    first = CTX // (2 * count) * 2 * index
    near = base[first + 1]
    base = base.at[first + 1].set(near)
    return jnp.clip(base, -6.375, 6.375)


def draw_cache_keys(key, part):
    keys = shared_keys(key)
    return keys.astype(jnp.bfloat16)


def draw_queries(key, part):
    key = jax.random.fold_in(key, 2)
    values = jax.random.normal(key, (NEW_TOKENS, HEADS * HEAD_DIM), jnp.float32)
    values = jnp.clip(1.6 * values, -6.4, 6.4)
    return values.astype(jnp.bfloat16)


def block_levels(rng, dims, split, least, largest):
    level, own = 1.0, jax.random.fold_in(rng, 6)
    for axis_at, shards_of in split:
        heights = jnp.exp(jax.random.uniform(jax.random.fold_in(own, axis_at), (shards_of,), jnp.float32, least / len(split), largest / len(split)))
        level = level * jnp.repeat(heights, dims[axis_at] // shards_of).reshape([-1 if axis == axis_at else 1 for axis in range(len(dims))])
    return level


def centred(key, extent, spread, most, shards=(), held_as=jnp.bfloat16):
    array = spread * jax.random.normal(key, extent, jnp.float32)
    if shards:
        array = array * block_levels(key, extent, shards, -0.22, 0.18)
    return jnp.clip(array, -most, most).astype(held_as)


def setup_inputs(seed: int = 0) -> dict:
    streams_of = jax.random.split(jax.random.key(seed), 7)
    return {
        "queries": draw_queries(jax.random.fold_in(streams_of[6], 71), 0),
        "cache_keys": draw_cache_keys(jax.random.fold_in(streams_of[6], 71), 0),
        "cache_values": centred(streams_of[2], (CTX, KV_HEADS * HEAD_DIM), 1.0, 6.0, ((0, 16), (1, 8))),
        "new_keys": centred(streams_of[3], (NEW_TOKENS, KV_HEADS * HEAD_DIM), 1.6, 6.375, ((0, 128),)),
        "new_values": centred(streams_of[4], (NEW_TOKENS, KV_HEADS * HEAD_DIM), 1.0, 6.0, ((0, 128),)),
        "sources": jax.random.permutation(streams_of[5], NEW_TOKENS).astype(jnp.int32),
    }


def owner_partial(queries, keys, values, key_pos, query_pos):
    group = HEADS // KV_HEADS
    scale = 1.0 / (HEAD_DIM ** 0.5)
    rows = queries.shape[0]
    outs = []
    lses = []
    for head in range(KV_HEADS):
        block = queries[:, head * group * HEAD_DIM:(head + 1) * group * HEAD_DIM].reshape(rows * group, HEAD_DIM)
        k_part = keys[:, head * HEAD_DIM:(head + 1) * HEAD_DIM]
        v_part = values[:, head * HEAD_DIM:(head + 1) * HEAD_DIM]
        scores = jnp.dot(block, k_part.T, preferred_element_type=jnp.float32) * scale
        row_pos = jnp.repeat(query_pos, group)
        allowed = key_pos[None, :] <= row_pos[:, None]
        scores = jnp.where(allowed, scores, jnp.float32(-1e30))
        peak = jnp.max(scores, axis=1)
        weight = jnp.exp(scores - peak[:, None])
        total = jnp.sum(weight, axis=1)
        mixed = jnp.dot(weight.astype(jnp.bfloat16), v_part, preferred_element_type=jnp.float32)
        outs.append((mixed / total[:, None]).astype(jnp.bfloat16).reshape(rows, group * HEAD_DIM))
        lses.append((peak + jnp.log(total)).reshape(rows, group))
    return jnp.concatenate(outs, axis=1), jnp.concatenate(lses, axis=1)


def reference(queries, cache_keys, cache_values, new_keys, new_values, sources):
    owners = NEW_TOKENS // NEW_DEV
    query_pos = (CTX + jnp.arange(NEW_TOKENS)).astype(jnp.int32)

    def visit(carry, owner):
        acc, running = carry
        start = (owner * CACHE_DEV).astype(jnp.int32)
        ck = lax.dynamic_slice_in_dim(cache_keys, start, CACHE_DEV, 0)
        cv = lax.dynamic_slice_in_dim(cache_values, start, CACHE_DEV, 0)
        slots = lax.dynamic_slice_in_dim(sources, (owner * NEW_DEV).astype(jnp.int32), NEW_DEV, 0)
        keys = jnp.concatenate([ck, jnp.take(new_keys, slots, axis=0)], axis=0)
        values = jnp.concatenate([cv, jnp.take(new_values, slots, axis=0)], axis=0)
        key_pos = jnp.concatenate([start + jnp.arange(CACHE_DEV).astype(jnp.int32), (CTX + slots).astype(jnp.int32)])
        part, lse = owner_partial(queries, keys, values, key_pos, query_pos)
        merged = jnp.logaddexp(running, lse)
        acc = acc * jnp.exp(running - merged)[:, :, None] + part.astype(jnp.float32).reshape(NEW_TOKENS, HEADS, HEAD_DIM) * jnp.exp(lse - merged)[:, :, None]
        return (acc, merged), None

    init = (jnp.zeros((NEW_TOKENS, HEADS, HEAD_DIM), jnp.float32), jnp.full((NEW_TOKENS, HEADS), -jnp.inf, jnp.float32))
    (acc, running), _ = lax.scan(visit, init, jnp.arange(owners).astype(jnp.int32))
    return acc.reshape(NEW_TOKENS, HEADS * HEAD_DIM).astype(jnp.bfloat16)
```

```python
import functools
import math

import jax
import jax.numpy as jnp
from jax import lax
from jax.experimental import pallas as pl
from jax.experimental.pallas import tpu as pltpu
from jax.sharding import PartitionSpec as P

HEAD_DIM = 128
GROUP = 16
OWNERS = 16
TP = 8
NEW = 128
CACHE = 1024
KEYS = CACHE + NEW
ROWS = NEW * GROUP
TILE = 1024
TILES = ROWS // TILE
MASKED = -1e30
SCALE = math.log2(math.e) / math.sqrt(HEAD_DIM)
MESH = pl.DeviceIdType.MESH
NT = (((1,), (1,)), ((), ()))
f32, bf16 = jnp.float32, jnp.bfloat16

CHIPS = [(0, 0), (-1, 0), (1, 0), (2, 0), (0, 1), (-1, 1), (1, 1), (2, 1)]
GROUP_OF = {chip: i for i, chip in enumerate(CHIPS)}


def kernel(
    q_ref, ck_ref, cv_ref, nk_ref, nv_ref, src_ref, o_ref,
    kc, vc, newt, kn, vn, lim, vtmp, stage, q2, sb, mb, pb, lb, mm, acc, den, top,
    local_sem, p1_send, p1_recv, p2_send, p2_recv, k_send, k_recv, v_send, v_recv,
):
    ctx, tp = lax.axis_index("ctx"), lax.axis_index("tp")
    x, yh, core = ((ctx) // 4), ((((ctx) // 2)) % 2), ((ctx) % 2)

    def owner_at(dx, dy, dc):
        return ((x + dx + 4) % 4) * 4 + ((yh + dy) % 2) * 2 + ((core + dc) % 2)

    def owner_of(slot):
        group = ((slot) // 2)
        place = ((group) % 4)
        dx = ((3 * place + (place // 2) * (2 * place - 5)) % 4)
        return owner_at(dx, ((group) // 4), ((slot) % 2))

    sibling = (owner_at(0, 0, 1), tp)
    right = (owner_at(1, 0, 0), tp)
    left = (owner_at(-1, 0, 0), tp)
    across = (owner_at(0, 1, 0), tp)

    def remote(src, dst, send, recv, to):
        return pltpu.make_async_remote_copy(
            src_ref=src, dst_ref=dst, send_sem=send, recv_sem=recv, device_id=to, device_id_type=MESH
        )

    barrier = pltpu.get_barrier_semaphore()
    peers = [(ctx, ((tp + d) % TP)) for d in range(1, TP)]
    peers += [(owner_at(dx, dy, 0), tp) for dx, dy in CHIPS[1:]] + [sibling]
    for peer in peers:
        pl.semaphore_signal(barrier, inc=1, device_id=peer, device_id_type=MESH)
    own_k = pltpu.make_async_copy(ck_ref, kc.at[0], local_sem.at[0])
    own_v = pltpu.make_async_copy(cv_ref, vtmp, local_sem.at[1])
    own_k.start()
    own_v.start()
    pl.semaphore_wait(barrier, len(peers))

    sends = []

    for d in range(1, TP):
        head = ((tp + d) % TP)
        cols = pl.ds(pl.multiple_of(head * HEAD_DIM, HEAD_DIM), HEAD_DIM)
        rows = pl.ds(pl.multiple_of(tp * 16, 16), 16)
        for i, ref in enumerate((nk_ref, nv_ref)):
            at = 2 * (d - 1) + i
            copy = remote(
                ref.at[:, cols], stage.at[i, rows, :], p1_send.at[at], p1_recv.at[at], (ctx, head)
            )
            copy.start()
            sends.append(copy)
    own_cols = pl.ds(pl.multiple_of(tp * HEAD_DIM, HEAD_DIM), HEAD_DIM)
    own_rows = pl.ds(pl.multiple_of(tp * 16, 16), 16)
    own_new = [
        pltpu.make_async_copy(ref.at[:, own_cols], stage.at[i, own_rows, :], local_sem.at[2 + i])
        for i, ref in enumerate((nk_ref, nv_ref))
    ]
    for copy in own_new:
        copy.start()

    def carrier(buf, send, recv):
        def go(at, src, dst, to):
            remote(buf.at[src], buf.at[dst], send.at[at], recv.at[dst], to).start()

        def landed(slot):
            pltpu.make_async_copy(buf.at[slot], buf.at[slot], recv.at[slot]).wait()

        def gone(at):
            pltpu.make_async_copy(buf.at[0], buf.at[0], send.at[at]).wait()

        return go, landed, gone

    go_k, landed_k, gone_k = carrier(kc, k_send, k_recv)
    go_v, landed_v, gone_v = carrier(vc, v_send, v_recv)
    go_n, landed_n, gone_n = carrier(newt, p2_send, p2_recv)

    own_k.wait()
    q_rows = []
    for h in range(GROUP):
        rows = pl.ds(h * NEW, NEW)
        part = q_ref[:, pl.ds(h * HEAD_DIM, HEAD_DIM)].astype(f32) * SCALE
        high = part.astype(bf16)
        q2[rows, :HEAD_DIM] = high
        q2[rows, HEAD_DIM:] = (part - high.astype(f32)).astype(bf16)
    for d in range(1, TP):
        for i in range(2):
            at = 2 * (d - 1) + i
            rows = pl.ds(pl.multiple_of(((tp - d + TP) % TP) * 16, 16), 16)
            pltpu.make_async_copy(stage.at[i, rows, :], stage.at[i, rows, :], p1_recv.at[at]).wait()
    for copy in own_new:
        copy.wait()
    newt[0, :HEAD_DIM, :] = stage[0].astype(f32).T.astype(bf16)
    newt[0, HEAD_DIM:, :] = stage[1].astype(f32).T.astype(bf16)
    for g in range(1, 8):
        dx, dy = CHIPS[g]
        back = GROUP_OF[(-dx if abs(dx) == 1 else dx, dy)]
        go_n(g, 0, 2 * back, (owner_at(dx, dy, 0), tp))
    go_n(0, 0, 1, sibling)
    go_k(0, 0, 1, sibling)
    go_k(1, 0, 2, right)
    go_k(2, 0, 4, left)
    go_k(3, 0, 8, across)
    own_v.wait()
    for b in range(CACHE // 128):
        vc[0, :, b * 128 : (b + 1) * 128] = vtmp[b * 128 : (b + 1) * 128, :].astype(f32).T.astype(bf16)
    go_v(0, 0, 1, sibling)
    go_v(1, 0, 2, right)
    go_v(2, 0, 4, left)
    go_v(3, 0, 8, across)

    acc[...] = jnp.zeros_like(acc)
    den[...] = jnp.zeros_like(den)
    top[...] = jnp.full_like(top, MASKED)

    def limits(slot, carry):
        owner = owner_of(slot)
        pos = jnp.broadcast_to(src_ref[pl.ds(owner, 1), :].astype(f32), (NEW, NEW)).T
        token = (ctx * NEW + lax.broadcasted_iota(jnp.int32, (NEW, NEW), 1)).astype(f32)
        lim[slot] = jnp.where(pos <= token, f32(3e38), f32(MASKED))
        return carry

    lax.fori_loop(0, OWNERS, limits, 0)

    def tile_queries(j):
        return q2[pl.ds(pl.multiple_of(j * TILE, TILE), TILE), :]

    def scores(keys, j):
        return lax.dot_general(
            jnp.concatenate([keys, keys], axis=1), tile_queries(j), NT, preferred_element_type=f32
        )

    def score_cached(slot, j):
        s = scores(kc[slot], j)
        sb[:CACHE, :] = s
        return jnp.max(s.reshape(CACHE // 8, 8, TILE), axis=0)

    def score_new(slot, j):
        bound = lim[slot]
        s = scores(kn[slot], j)
        s = jnp.minimum(s, jnp.concatenate([bound] * (TILE // NEW), axis=1))
        sb[CACHE:, :] = s
        return jnp.max(s.reshape(NEW // 8, 8, TILE), axis=0)

    def score(slot, j):
        mb[...] = jnp.maximum(score_cached(slot, j), score_new(slot, j))

    def weigh():
        peak = jnp.max(mb[...], axis=0, keepdims=True)
        total = None
        for at in range(0, KEYS, 128):
            w = jnp.exp2(sb[at : at + 128, :] - peak)
            part = jnp.sum(w.reshape(16, 8, TILE), axis=0)
            total = part if total is None else total + part
            pb[at : at + 128, :] = w.astype(bf16)
        lb[...] = jnp.sum(total, axis=0, keepdims=True)
        mm[...] = peak

    def mix(slot, j):
        total, peak = lb[...], mm[...]
        values = jnp.concatenate([vc[slot], vn[slot]], axis=1)
        mixed = jnp.dot(values, pb[...], preferred_element_type=f32)
        partial = (mixed * (1.0 / total)).astype(bf16).astype(f32)
        lse = peak + jnp.log2(total)
        old = top[j]
        new = jnp.maximum(old, lse)
        keep, add = jnp.exp2(old - new), jnp.exp2(lse - new)
        acc[j] = acc[j] * keep + partial * add
        den[j] = den[j] * keep + add
        top[j] = new

    mb[...] = score_cached(0, 0)

    for g in range(1, 8):
        landed_n(2 * g)
        go_n(7 + g, 2 * g, 2 * g + 1, sibling)
    landed_n(1)
    for g in range(1, 8):
        landed_n(2 * g + 1)

    def pick(pair, carry):
        want = jnp.concatenate(
            [src_ref[pl.ds(owner_of(2 * pair + i), 1), :] for i in range(2)], axis=1
        )
        hot, rows = [], []
        for slot in range(OWNERS):
            dx, dy = CHIPS[slot // 2]
            token = owner_at(dx, dy, slot % 2) * NEW + lax.broadcasted_iota(jnp.int32, (NEW, 2 * NEW), 0)
            hot.append(jnp.where(token == want, f32(1), f32(0)).astype(bf16))
            rows.append(newt[slot])
        got = jnp.dot(
            jnp.concatenate(rows, axis=1), jnp.concatenate(hot, axis=0), preferred_element_type=f32
        )
        for i in range(2):
            cols = slice(i * NEW, (i + 1) * NEW)
            kn[2 * pair + i] = got[:HEAD_DIM, cols].T.astype(bf16)
            vn[2 * pair + i] = got[HEAD_DIM:, cols].astype(bf16)
        return carry

    lax.fori_loop(0, OWNERS // 2, pick, 0)

    mb[...] = jnp.maximum(mb[...], score_new(0, 0))
    weigh()
    score(0, 1)

    def relay(t):
        @pl.when(t == 0)
        def _():
            landed_k(1)
            landed_v(1)

        @pl.when(t == 1)
        def _():
            landed_k(2)
            go_k(4, 2, 6, right)
            go_k(5, 2, 3, sibling)
            landed_k(4)
            go_k(6, 4, 5, sibling)
            landed_k(8)
            go_k(7, 8, 10, right)
            go_k(8, 8, 12, left)
            go_k(9, 8, 9, sibling)

        @pl.when(t == 3)
        def _():
            landed_v(2)
            go_v(4, 2, 3, sibling)
            landed_v(4)
            go_v(5, 4, 6, left)
            go_v(6, 4, 5, sibling)
            landed_v(8)
            go_v(7, 8, 10, right)
            go_v(8, 8, 12, left)
            go_v(9, 8, 9, sibling)

        @pl.when(t == 4)
        def _():
            landed_k(3)

        @pl.when(t == 6)
        def _():
            landed_v(3)

        @pl.when(t == 8)
        def _():
            landed_k(5)
            landed_v(5)
            landed_k(6)
            go_k(10, 6, 7, sibling)
            landed_v(6)
            go_v(10, 6, 7, sibling)

        @pl.when(t == 11)
        def _():
            landed_k(10)
            go_k(11, 10, 14, right)
            go_k(12, 10, 11, sibling)
            landed_k(12)
            go_k(13, 12, 13, sibling)
            landed_v(10)
            go_v(11, 10, 11, sibling)
            landed_v(12)
            go_v(12, 12, 14, left)
            go_v(13, 12, 13, sibling)

        @pl.when(t == 12)
        def _():
            landed_k(7)
            landed_v(7)

        @pl.when(t == 16)
        def _():
            landed_k(9)
            landed_v(9)

        @pl.when(t == 20)
        def _():
            landed_k(11)
            landed_v(11)

        @pl.when(t == 22)
        def _():
            landed_k(14)
            go_k(14, 14, 15, sibling)
            landed_v(14)
            go_v(14, 14, 15, sibling)

        @pl.when(t == 24)
        def _():
            landed_k(13)
            landed_v(13)

        @pl.when(t == 28)
        def _():
            landed_k(15)
            landed_v(15)

    def step(t, carry):
        relay(t)
        mix(((t) // TILES), ((t) % TILES))
        weigh()
        score(((t + 2) // TILES), ((t + 2) % TILES))
        return carry

    last = OWNERS * TILES
    lax.fori_loop(0, last - 2, step, 0)
    mix(OWNERS - 1, TILES - 2)
    weigh()
    mix(OWNERS - 1, TILES - 1)

    per = TILE // NEW
    for h in range(GROUP):
        j, at = h // per, (h % per) * NEW
        part = acc[j, :, at : at + NEW] * (1.0 / den[j, :, at : at + NEW])
        o_ref[:, h * HEAD_DIM : (h + 1) * HEAD_DIM] = part.T.astype(bf16)

    for copy in sends:
        copy.wait_send()
    for at in range(15):
        gone_n(at)
        gone_k(at)
        gone_v(at)


def on_device(queries, cache_keys, cache_values, new_keys, new_values, sources):
    vmem, dma = pltpu.VMEM, pltpu.SemaphoreType.DMA
    whole = pl.BlockSpec(memory_space=pltpu.VMEM)
    there = pl.BlockSpec(memory_space=pl.ANY)
    return pl.pallas_call(
        kernel,
        out_shape=jax.ShapeDtypeStruct(queries.shape, queries.dtype),
        in_specs=[whole, there, there, whole, whole, whole],
        out_specs=whole,
        scratch_shapes=[
            vmem((OWNERS, CACHE, HEAD_DIM), bf16),
            vmem((OWNERS, HEAD_DIM, CACHE), bf16),
            vmem((OWNERS, 2 * HEAD_DIM, NEW), bf16),
            vmem((OWNERS, NEW, HEAD_DIM), bf16),
            vmem((OWNERS, HEAD_DIM, NEW), bf16),
            vmem((OWNERS, NEW, NEW), f32),
            vmem((CACHE, HEAD_DIM), bf16),
            vmem((2, NEW, HEAD_DIM), bf16),
            vmem((ROWS, 2 * HEAD_DIM), bf16),
            vmem((KEYS, TILE), f32),
            vmem((8, TILE), f32),
            vmem((KEYS, TILE), bf16),
            vmem((1, TILE), f32),
            vmem((1, TILE), f32),
            vmem((TILES, HEAD_DIM, TILE), f32),
            vmem((TILES, 1, TILE), f32),
            vmem((TILES, 1, TILE), f32),
            dma((4,)),
            dma((14,)),
            dma((14,)),
            dma((15,)),
            dma((OWNERS,)),
            dma((15,)),
            dma((OWNERS,)),
            dma((15,)),
            dma((OWNERS,)),
        ],
        compiler_params=pltpu.CompilerParams(
            collective_id=0, has_side_effects=True, vmem_limit_bytes=60 * 2**20
        ),
    )(queries, cache_keys, cache_values, new_keys, new_values, sources.reshape(OWNERS, NEW))


def solution(mesh):
    placed = (
        P("ctx", "tp"),
        P("ctx", "tp"),
        P("ctx", "tp"),
        P(("ctx", "tp"), None),
        P(("ctx", "tp"), None),
        P(),
    )
    return jax.shard_map(on_device, mesh=mesh, in_specs=placed, out_specs=P("ctx", "tp"), check_vma=False)
```

```python
import functools
import math

import jax
import jax.numpy as jnp
from jax import lax
from jax.experimental import pallas as pl
from jax.experimental.pallas import tpu as pltpu
from jax.sharding import PartitionSpec as P

HEAD_DIM = 128
GROUP = 16
OWNERS = 16
TP = 8
NEW = 128
CACHE = 1024
KEYS = CACHE + NEW
ROWS = NEW * GROUP
TILE = 1024
TILES = ROWS // TILE
WIDE = 256
SPLITS = TILE // WIDE
MASKED = -1e30
SCALE = math.log2(math.e) / math.sqrt(HEAD_DIM)
MESH = pl.DeviceIdType.MESH
NT = (((1,), (1,)), ((), ()))
f32, bf16 = jnp.float32, jnp.bfloat16

CHIPS = [(0, 0), (-1, 0), (1, 0), (2, 0), (0, 1), (-1, 1), (1, 1), (2, 1)]
GROUP_OF = {chip: i for i, chip in enumerate(CHIPS)}


def kernel(
    q_ref, ck_ref, cv_ref, nk_ref, nv_ref, src_ref, o_ref,
    kc, vc, newt, kn, vn, lim, hot, vtmp, pack, stage, q2, sb, mb, pb, lb, mm, acc, den, top,
    local_sem, p1_send, p1_recv, p2_send, p2_recv, k_send, k_recv, v_send, v_recv,
):
    ctx, tp = lax.axis_index("ctx"), lax.axis_index("tp")
    x, yh, core = ctx // 4, (ctx // 2) % 2, ctx % 2

    def owner_at(dx, dy, dc):
        return ((x + dx + 4) % 4) * 4 + ((yh + dy) % 2) * 2 + (core + dc) % 2

    def owner_of(slot):
        group = slot // 2
        place = group % 4
        dx = (3 * place + (place // 2) * (2 * place - 5)) % 4
        return owner_at(dx, group // 4, slot % 2)

    sibling = (owner_at(0, 0, 1), tp)
    right = (owner_at(1, 0, 0), tp)
    left = (owner_at(-1, 0, 0), tp)
    across = (owner_at(0, 1, 0), tp)

    def remote(src, dst, send, recv, to):
        return pltpu.make_async_remote_copy(
            src_ref=src, dst_ref=dst, send_sem=send, recv_sem=recv, device_id=to, device_id_type=MESH
        )

    def carrier(buf, send, recv):
        def go(at, src, dst, to):
            remote(buf.at[src], buf.at[dst], send.at[at], recv.at[dst], to).start()

        def landed(slot):
            pltpu.make_async_copy(buf.at[slot], buf.at[slot], recv.at[slot]).wait()

        def gone(at):
            pltpu.make_async_copy(buf.at[0], buf.at[0], send.at[at]).wait()

        return go, landed, gone

    go_k, landed_k, gone_k = carrier(kc, k_send, k_recv)
    go_v, landed_v, gone_v = carrier(vc, v_send, v_recv)
    go_n, landed_n, gone_n = carrier(newt, p2_send, p2_recv)

    barrier = pltpu.get_barrier_semaphore()
    peers = [(ctx, (tp + d) % TP) for d in range(1, TP)]
    peers += [(owner_at(dx, dy, 0), tp) for dx, dy in CHIPS[1:]] + [sibling]
    for peer in peers:
        pl.semaphore_signal(barrier, inc=1, device_id=peer, device_id_type=MESH)

    own_k = pltpu.make_async_copy(ck_ref, kc.at[0], local_sem.at[0])
    own_v = pltpu.make_async_copy(cv_ref, vtmp, local_sem.at[1])
    own_k.start()
    own_v.start()
    for h in range(TP):
        cols = slice(h * HEAD_DIM, (h + 1) * HEAD_DIM)
        pack[h, :16, :] = nk_ref[:, cols]
        pack[h, 16:, :] = nv_ref[:, cols]
    stage[tp] = pack[tp]
    own_k.wait()

    pl.semaphore_wait(barrier, len(peers))
    for d in range(1, TP):
        head = (tp + d) % TP
        remote(pack.at[head], stage.at[tp], p1_send.at[d - 1], p1_recv.at[d - 1], (ctx, head)).start()
    go_k(0, 0, 1, sibling)
    go_k(1, 0, 2, right)
    go_k(2, 0, 4, left)

    for h in range(GROUP):
        rows = pl.ds(h * NEW, NEW)
        part = q_ref[:, pl.ds(h * HEAD_DIM, HEAD_DIM)].astype(f32) * SCALE
        high = part.astype(bf16)
        q2[rows, :HEAD_DIM] = high
        q2[rows, HEAD_DIM:] = (part - high.astype(f32)).astype(bf16)
    own_v.wait()
    for b in range(CACHE // 128):
        vc[0, :, b * 128 : (b + 1) * 128] = vtmp[b * 128 : (b + 1) * 128, :].astype(f32).T.astype(bf16)
    go_v(0, 0, 1, sibling)
    acc[...] = jnp.zeros_like(acc)
    den[...] = jnp.zeros_like(den)
    top[...] = jnp.full_like(top, MASKED)

    def limits(slot, carry):
        owner = owner_of(slot)
        pos = jnp.broadcast_to(src_ref[pl.ds(owner, 1), :].astype(f32), (NEW, NEW)).T
        token = (ctx * NEW + lax.broadcasted_iota(jnp.int32, (NEW, NEW), 1)).astype(f32)
        lim[slot] = jnp.where(pos <= token, f32(3e38), f32(MASKED))
        return carry

    lax.fori_loop(0, OWNERS, limits, 0)

    def columns(c):
        return pl.ds(c * WIDE, WIDE)

    def scores(keys, j, c):
        queries = q2[pl.ds(pl.multiple_of(j * TILE + c * WIDE, WIDE), WIDE), :]
        return lax.dot_general(
            jnp.concatenate([keys, keys], axis=1), queries, NT, preferred_element_type=f32
        )

    def peaks(s):
        return jnp.max(s.reshape(s.shape[0] // 8, 8, WIDE), axis=0)

    def masked(s, slot):
        return jnp.minimum(s, jnp.concatenate([lim[slot]] * (WIDE // NEW), axis=1))

    def score(slot, j, c):
        s = scores(jnp.concatenate([kc[slot], kn[slot]], axis=0), j, c)
        cached, new = s[:CACHE], masked(s[CACHE:], slot)
        sb[:CACHE, columns(c)] = cached
        sb[CACHE:, columns(c)] = new
        mb[:, columns(c)] = jnp.maximum(peaks(cached), peaks(new))

    def weigh(c):
        cols = columns(c)
        peak = jnp.max(mb[:, cols], axis=0, keepdims=True)
        total = None
        for at in range(0, KEYS, 128):
            w = jnp.exp2(sb[at : at + 128, cols] - peak)
            part = jnp.sum(w.reshape(16, 8, WIDE), axis=0)
            total = part if total is None else total + part
            pb[at : at + 128, cols] = w.astype(bf16)
        lb[:, cols] = jnp.sum(total, axis=0, keepdims=True)
        mm[:, cols] = peak

    def mix(slot, j, c):
        cols = columns(c)
        total, peak = lb[:, cols], mm[:, cols]
        values = jnp.concatenate([vc[slot], vn[slot]], axis=1)
        mixed = jnp.dot(values, pb[:, cols], preferred_element_type=f32)
        partial = (mixed * (1.0 / total)).astype(bf16).astype(f32)
        lse = peak + jnp.log2(total)
        old = top[j, :, cols]
        new = jnp.maximum(old, lse)
        keep, add = jnp.exp2(old - new), jnp.exp2(lse - new)
        acc[j, :, cols] = acc[j, :, cols] * keep + partial * add
        den[j, :, cols] = den[j, :, cols] * keep + add
        top[j, :, cols] = new

    for c in range(SPLITS):
        s = scores(kc[0], 0, c)
        sb[:CACHE, columns(c)] = s
        mb[:, columns(c)] = peaks(s)

    for d in range(1, TP):
        source = (tp - d + TP) % TP
        pltpu.make_async_copy(stage.at[source], stage.at[source], p1_recv.at[d - 1]).wait()
    for i in range(2):
        rows = jnp.concatenate([stage[h, i * 16 : (i + 1) * 16, :] for h in range(TP)], axis=0)
        newt[0, i * HEAD_DIM : (i + 1) * HEAD_DIM, :] = rows.astype(f32).T.astype(bf16)
    for g in (4, 7, 5, 6, 3, 1, 2):
        dx, dy = CHIPS[g]
        back = GROUP_OF[(-dx if abs(dx) == 1 else dx, dy)]
        go_n(g, 0, 2 * back, (owner_at(dx, dy, 0), tp))
    go_n(0, 0, 1, sibling)
    go_k(3, 0, 8, across)

    def choose(pair, carry):
        want = jnp.concatenate(
            [src_ref[pl.ds(owner_of(2 * pair + i), 1), :] for i in range(2)], axis=1
        )
        for slot in range(OWNERS):
            dx, dy = CHIPS[slot // 2]
            token = owner_at(dx, dy, slot % 2) * NEW + lax.broadcasted_iota(jnp.int32, (NEW, 2 * NEW), 0)
            rows = slice(slot * NEW, (slot + 1) * NEW)
            hot[pair, rows, :] = jnp.where(token == want, f32(1), f32(0)).astype(bf16)
        return carry

    lax.fori_loop(0, OWNERS // 2, choose, 0)

    for g in (1, 2, 3, 4, 5, 6, 7):
        landed_n(2 * g)
        go_n(7 + g, 2 * g, 2 * g + 1, sibling)
    go_v(1, 0, 2, right)
    go_v(2, 0, 4, left)
    go_v(3, 0, 8, across)
    landed_k(2)
    go_k(4, 2, 6, right)
    go_k(5, 2, 3, sibling)
    landed_k(4)
    go_k(6, 4, 5, sibling)
    landed_n(1)
    for g in range(1, 8):
        landed_n(2 * g + 1)

    def pick(pair):
        rows = jnp.concatenate([newt[slot] for slot in range(OWNERS)], axis=1)
        got = jnp.dot(rows, hot[pair], preferred_element_type=f32)
        for i in range(2):
            cols = slice(i * NEW, (i + 1) * NEW)
            kn[2 * pair + i] = got[:HEAD_DIM, cols].T.astype(bf16)
            vn[2 * pair + i] = got[HEAD_DIM:, cols].astype(bf16)

    pick(0)
    for c in range(SPLITS):
        s = masked(scores(kn[0], 0, c), 0)
        sb[CACHE:, columns(c)] = s
        mb[:, columns(c)] = jnp.maximum(mb[:, columns(c)], peaks(s))
    for i in range(SPLITS + 1):
        if i >= 1:
            score(0, 1, i - 1)
        if i < SPLITS:
            weigh(i)

    def relay(t):
        @pl.when((t % 4 == 1) & (t < 4 * 7))
        def _():
            pick(t // 4 + 1)

        @pl.when(t == 0)
        def _():
            landed_k(1)
            landed_v(1)

        @pl.when(t == 4)
        def _():
            landed_k(3)
            landed_v(2)
            go_v(4, 2, 3, sibling)
            landed_v(4)
            go_v(5, 4, 6, left)
            go_v(6, 4, 5, sibling)

        @pl.when(t == 5)
        def _():
            landed_k(8)
            go_k(7, 8, 10, right)
            go_k(8, 8, 12, left)
            go_k(9, 8, 9, sibling)

        @pl.when(t == 6)
        def _():
            landed_v(3)

        @pl.when(t == 8)
        def _():
            landed_k(5)
            landed_v(5)

        @pl.when(t == 9)
        def _():
            landed_v(8)
            go_v(7, 8, 10, right)
            go_v(8, 8, 12, left)
            go_v(9, 8, 9, sibling)
            landed_k(6)
            go_k(10, 6, 7, sibling)

        @pl.when(t == 11)
        def _():
            landed_v(6)
            go_v(10, 6, 7, sibling)

        @pl.when(t == 12)
        def _():
            landed_k(7)

        @pl.when(t == 14)
        def _():
            landed_v(7)
            landed_k(10)
            go_k(11, 10, 14, right)
            go_k(12, 10, 11, sibling)
            landed_k(12)
            go_k(13, 12, 13, sibling)

        @pl.when(t == 16)
        def _():
            landed_k(9)
            landed_v(9)

        @pl.when(t == 17)
        def _():
            landed_v(10)
            go_v(11, 10, 11, sibling)
            landed_v(12)
            go_v(12, 12, 14, left)
            go_v(13, 12, 13, sibling)

        @pl.when(t == 20)
        def _():
            landed_k(11)

        @pl.when(t == 22)
        def _():
            landed_v(11)
            landed_k(14)
            go_k(14, 14, 15, sibling)
            landed_v(14)
            go_v(14, 14, 15, sibling)

        @pl.when(t == 24)
        def _():
            landed_k(13)
            landed_v(13)

        @pl.when(t == 28)
        def _():
            landed_k(15)
            landed_v(15)

    def step(t, carry):
        relay(t)
        for i in range(SPLITS + 2):
            if i >= 2:
                score((t + 2) // TILES, (t + 2) % TILES, i - 2)
            if 1 <= i <= SPLITS:
                weigh(i - 1)
            if i < SPLITS:
                mix(t // TILES, t % TILES, i)
        return carry

    lax.fori_loop(0, OWNERS * TILES - 2, step, 0)
    for i in range(SPLITS + 1):
        if i >= 1:
            weigh(i - 1)
        if i < SPLITS:
            mix(OWNERS - 1, TILES - 2, i)
    for c in range(SPLITS):
        mix(OWNERS - 1, TILES - 1, c)

    per = TILE // NEW
    for h in range(GROUP):
        j, at = h // per, (h % per) * NEW
        part = acc[j, :, at : at + NEW] * (1.0 / den[j, :, at : at + NEW])
        o_ref[:, h * HEAD_DIM : (h + 1) * HEAD_DIM] = part.T.astype(bf16)

    for d in range(1, TP):
        pltpu.make_async_copy(pack.at[0], pack.at[0], p1_send.at[d - 1]).wait()
    for at in range(15):
        gone_n(at)
        gone_k(at)
        gone_v(at)


def on_device(queries, cache_keys, cache_values, new_keys, new_values, sources):
    vmem, dma = pltpu.VMEM, pltpu.SemaphoreType.DMA
    whole = pl.BlockSpec(memory_space=pltpu.VMEM)
    there = pl.BlockSpec(memory_space=pl.ANY)
    return pl.pallas_call(
        kernel,
        out_shape=jax.ShapeDtypeStruct(queries.shape, queries.dtype),
        in_specs=[whole, there, there, whole, whole, whole],
        out_specs=whole,
        scratch_shapes=[
            vmem((OWNERS, CACHE, HEAD_DIM), bf16),
            vmem((OWNERS, HEAD_DIM, CACHE), bf16),
            vmem((OWNERS, 2 * HEAD_DIM, NEW), bf16),
            vmem((OWNERS, NEW, HEAD_DIM), bf16),
            vmem((OWNERS, HEAD_DIM, NEW), bf16),
            vmem((OWNERS, NEW, NEW), f32),
            vmem((OWNERS // 2, OWNERS * NEW, 2 * NEW), bf16),
            vmem((CACHE, HEAD_DIM), bf16),
            vmem((TP, 32, HEAD_DIM), bf16),
            vmem((TP, 32, HEAD_DIM), bf16),
            vmem((ROWS, 2 * HEAD_DIM), bf16),
            vmem((KEYS, TILE), f32),
            vmem((8, TILE), f32),
            vmem((KEYS, TILE), bf16),
            vmem((1, TILE), f32),
            vmem((1, TILE), f32),
            vmem((TILES, HEAD_DIM, TILE), f32),
            vmem((TILES, 1, TILE), f32),
            vmem((TILES, 1, TILE), f32),
            dma((2,)),
            dma((7,)),
            dma((7,)),
            dma((15,)),
            dma((OWNERS,)),
            dma((15,)),
            dma((OWNERS,)),
            dma((15,)),
            dma((OWNERS,)),
        ],
        compiler_params=pltpu.CompilerParams(
            collective_id=0, has_side_effects=True, vmem_limit_bytes=60 * 2**20
        ),
    )(queries, cache_keys, cache_values, new_keys, new_values, sources.reshape(OWNERS, NEW))


def solution(mesh):
    placed = (
        P("ctx", "tp"),
        P("ctx", "tp"),
        P("ctx", "tp"),
        P(("ctx", "tp"), None),
        P(("ctx", "tp"), None),
        P(),
    )
    return jax.shard_map(on_device, mesh=mesh, in_specs=placed, out_specs=P("ctx", "tp"), check_vma=False)
```

```python
import functools
import math

import jax
import jax.numpy as jnp
from jax import lax
from jax.experimental import pallas as pl
from jax.experimental.pallas import tpu as pltpu
from jax.sharding import PartitionSpec as P

HEAD_DIM = 128
GROUP = 16
OWNERS = 16
TP = 8
NEW = 128
CACHE = 1024
KEYS = CACHE + NEW
ROWS = NEW * GROUP
TILE = 1024
TILES = ROWS // TILE
WIDE = 256
SPLITS = TILE // WIDE
MASKED = -1e30
SCALE = math.log2(math.e) / math.sqrt(HEAD_DIM)
MESH = pl.DeviceIdType.MESH
NT = (((1,), (1,)), ((), ()))
f32, bf16 = jnp.float32, jnp.bfloat16

CHIPS = [(0, 0), (-1, 0), (1, 0), (2, 0), (0, 1), (-1, 1), (1, 1), (2, 1)]
GROUP_OF = {chip: i for i, chip in enumerate(CHIPS)}


def kernel(
    q_ref, ck_ref, cv_ref, nk_ref, nv_ref, src_ref, o_ref,
    kc, vc, newt, kn, vn, lim, hot, vtmp, pack, stage, q2, sb, mb, pb, lb, mm, acc, den, top,
    local_sem, p1_send, p1_recv, p2_send, p2_recv, k_send, k_recv, v_send, v_recv,
):
    ctx, tp = lax.axis_index("ctx"), lax.axis_index("tp")
    x, yh, core = ctx // 4, (ctx // 2) % 2, ctx % 2

    def owner_at(dx, dy, dc):
        return ((x + dx + 4) % 4) * 4 + ((yh + dy) % 2) * 2 + (core + dc) % 2

    def owner_of(slot):
        group = slot // 2
        place = group % 4
        dx = (3 * place + (place // 2) * (2 * place - 5)) % 4
        return owner_at(dx, group // 4, slot % 2)

    sibling = (owner_at(0, 0, 1), tp)
    right = (owner_at(1, 0, 0), tp)
    left = (owner_at(-1, 0, 0), tp)
    across = (owner_at(0, 1, 0), tp)

    def remote(src, dst, send, recv, to):
        return pltpu.make_async_remote_copy(
            src_ref=src, dst_ref=dst, send_sem=send, recv_sem=recv, device_id=to, device_id_type=MESH
        )

    def carrier(buf, send, recv):
        def go(at, src, dst, to):
            remote(buf.at[src], buf.at[dst], send.at[at], recv.at[dst], to).start()

        def landed(slot):
            pltpu.make_async_copy(buf.at[slot], buf.at[slot], recv.at[slot]).wait()

        def gone(at):
            pltpu.make_async_copy(buf.at[0], buf.at[0], send.at[at]).wait()

        return go, landed, gone

    go_k, landed_k, gone_k = carrier(kc, k_send, k_recv)
    go_v, landed_v, gone_v = carrier(vc, v_send, v_recv)
    go_n, landed_n, gone_n = carrier(newt, p2_send, p2_recv)

    barrier = pltpu.get_barrier_semaphore()
    peers = [(ctx, (tp + d) % TP) for d in range(1, TP)]
    peers += [(owner_at(dx, dy, 0), tp) for dx, dy in CHIPS[1:]] + [sibling]
    for peer in peers:
        pl.semaphore_signal(barrier, inc=1, device_id=peer, device_id_type=MESH)

    own_k = pltpu.make_async_copy(ck_ref, kc.at[0], local_sem.at[0])
    own_v = pltpu.make_async_copy(cv_ref, vtmp, local_sem.at[1])
    own_k.start()
    own_v.start()
    for h in range(TP):
        cols = slice(h * HEAD_DIM, (h + 1) * HEAD_DIM)
        pack[h, :16, :] = nk_ref[:, cols]
        pack[h, 16:, :] = nv_ref[:, cols]
    stage[tp] = pack[tp]
    own_k.wait()

    pl.semaphore_wait(barrier, len(peers))
    for d in range(1, TP):
        head = (tp + d) % TP
        remote(pack.at[head], stage.at[tp], p1_send.at[d - 1], p1_recv.at[d - 1], (ctx, head)).start()
    go_k(0, 0, 1, sibling)
    go_k(1, 0, 2, right)
    go_k(2, 0, 4, left)

    for h in range(GROUP):
        rows = pl.ds(h * NEW, NEW)
        part = q_ref[:, pl.ds(h * HEAD_DIM, HEAD_DIM)].astype(f32) * SCALE
        high = part.astype(bf16)
        q2[rows, :HEAD_DIM] = high
        q2[rows, HEAD_DIM:] = (part - high.astype(f32)).astype(bf16)
    own_v.wait()
    for b in range(CACHE // 128):
        vc[0, :, b * 128 : (b + 1) * 128] = vtmp[b * 128 : (b + 1) * 128, :].astype(f32).T.astype(bf16)
    go_v(0, 0, 1, sibling)
    acc[...] = jnp.zeros_like(acc)
    den[...] = jnp.zeros_like(den)
    top[...] = jnp.full_like(top, MASKED)

    def limits(slot, carry):
        owner = owner_of(slot)
        pos = jnp.broadcast_to(src_ref[pl.ds(owner, 1), :].astype(f32), (NEW, NEW)).T
        token = (ctx * NEW + lax.broadcasted_iota(jnp.int32, (NEW, NEW), 1)).astype(f32)
        lim[slot] = jnp.where(pos <= token, f32(3e38), f32(MASKED))
        return carry

    lax.fori_loop(0, OWNERS, limits, 0)

    def columns(c):
        return pl.ds(c * WIDE, WIDE)

    def scores(keys, j, c):
        queries = q2[pl.ds(pl.multiple_of(j * TILE + c * WIDE, WIDE), WIDE), :]
        return lax.dot_general(
            jnp.concatenate([keys, keys], axis=1), queries, NT, preferred_element_type=f32
        )

    def peaks(s):
        return jnp.max(s.reshape(s.shape[0] // 8, 8, WIDE), axis=0)

    def masked(s, slot):
        return jnp.minimum(s, jnp.concatenate([lim[slot]] * (WIDE // NEW), axis=1))

    def score(slot, j, c):
        s = scores(jnp.concatenate([kc[slot], kn[slot]], axis=0), j, c)
        cached, new = s[:CACHE], masked(s[CACHE:], slot)
        sb[:CACHE, columns(c)] = cached
        sb[CACHE:, columns(c)] = new
        mb[:, columns(c)] = jnp.maximum(peaks(cached), peaks(new))

    def weigh(c):
        cols = columns(c)
        peak = jnp.max(mb[:, cols], axis=0, keepdims=True)
        total = None
        for at in range(0, KEYS, 128):
            w = jnp.exp2(sb[at : at + 128, cols] - peak)
            part = jnp.sum(w.reshape(16, 8, WIDE), axis=0)
            total = part if total is None else total + part
            pb[at : at + 128, cols] = w.astype(bf16)
        lb[:, cols] = jnp.sum(total, axis=0, keepdims=True)
        mm[:, cols] = peak

    def mix(slot, j, c):
        cols = columns(c)
        total, peak = lb[:, cols], mm[:, cols]
        values = jnp.concatenate([vc[slot], vn[slot]], axis=1)
        mixed = jnp.dot(values, pb[:, cols], preferred_element_type=f32)
        partial = (mixed * (1.0 / total)).astype(bf16).astype(f32)
        lse = peak + jnp.log2(total)
        old = top[j, :, cols]
        new = jnp.maximum(old, lse)
        keep, add = jnp.exp2(old - new), jnp.exp2(lse - new)
        acc[j, :, cols] = acc[j, :, cols] * keep + partial * add
        den[j, :, cols] = den[j, :, cols] * keep + add
        top[j, :, cols] = new

    for c in range(SPLITS):
        s = scores(kc[0], 0, c)
        sb[:CACHE, columns(c)] = s
        mb[:, columns(c)] = peaks(s)

    for d in range(1, TP):
        source = (tp - d + TP) % TP
        pltpu.make_async_copy(stage.at[source], stage.at[source], p1_recv.at[d - 1]).wait()
    for i in range(2):
        rows = jnp.concatenate([stage[h, i * 16 : (i + 1) * 16, :] for h in range(TP)], axis=0)
        newt[0, i * HEAD_DIM : (i + 1) * HEAD_DIM, :] = rows.astype(f32).T.astype(bf16)
    for g in (4, 7, 5, 6, 3, 1, 2):
        dx, dy = CHIPS[g]
        back = GROUP_OF[(-dx if abs(dx) == 1 else dx, dy)]
        go_n(g, 0, 2 * back, (owner_at(dx, dy, 0), tp))
    go_n(0, 0, 1, sibling)
    go_v(1, 0, 2, right)
    go_v(2, 0, 4, left)
    go_k(3, 0, 8, across)

    def choose(pair, carry):
        want = jnp.concatenate(
            [src_ref[pl.ds(owner_of(2 * pair + i), 1), :] for i in range(2)], axis=1
        )
        for slot in range(OWNERS):
            dx, dy = CHIPS[slot // 2]
            token = owner_at(dx, dy, slot % 2) * NEW + lax.broadcasted_iota(jnp.int32, (NEW, 2 * NEW), 0)
            rows = slice(slot * NEW, (slot + 1) * NEW)
            hot[pair, rows, :] = jnp.where(token == want, f32(1), f32(0)).astype(bf16)
        return carry

    lax.fori_loop(0, OWNERS // 2, choose, 0)

    for g in (1, 2, 3, 4, 5, 6, 7):
        landed_n(2 * g)
        go_n(7 + g, 2 * g, 2 * g + 1, sibling)
    go_v(3, 0, 8, across)
    landed_k(2)
    go_k(4, 2, 6, right)
    go_k(5, 2, 3, sibling)
    landed_k(4)
    go_k(6, 4, 5, sibling)
    landed_n(1)
    for g in range(1, 8):
        landed_n(2 * g + 1)

    def pick(pair):
        rows = jnp.concatenate([newt[slot] for slot in range(OWNERS)], axis=1)
        got = jnp.dot(rows, hot[pair], preferred_element_type=f32)
        for i in range(2):
            cols = slice(i * NEW, (i + 1) * NEW)
            kn[2 * pair + i] = got[:HEAD_DIM, cols].T.astype(bf16)
            vn[2 * pair + i] = got[HEAD_DIM:, cols].astype(bf16)

    pick(0)
    for c in range(SPLITS):
        s = masked(scores(kn[0], 0, c), 0)
        sb[CACHE:, columns(c)] = s
        mb[:, columns(c)] = jnp.maximum(mb[:, columns(c)], peaks(s))
    for i in range(SPLITS + 1):
        if i >= 1:
            score(0, 1, i - 1)
        if i < SPLITS:
            weigh(i)

    def relay(slot):
        @pl.when(slot % 2 == 1)
        def _():
            pick((slot + 1) // 2)

        @pl.when(slot == 0)
        def _():
            landed_k(1)
            landed_v(1)

        @pl.when(slot == 1)
        def _():
            landed_v(2)
            go_v(4, 2, 3, sibling)
            landed_v(4)
            go_v(5, 4, 6, left)
            go_v(6, 4, 5, sibling)
            landed_k(8)
            go_k(7, 8, 10, right)
            go_k(8, 8, 12, left)
            go_k(9, 8, 9, sibling)

        @pl.when(slot == 2)
        def _():
            landed_k(3)

        @pl.when(slot == 3)
        def _():
            landed_v(3)
            landed_k(6)
            go_k(10, 6, 14, across)
            go_k(11, 6, 7, sibling)
            landed_v(8)
            go_v(7, 8, 10, right)
            go_v(8, 8, 12, left)
            go_v(9, 8, 9, sibling)

        @pl.when(slot == 4)
        def _():
            landed_k(5)
            landed_v(5)
            landed_v(6)
            go_v(10, 6, 14, across)
            go_v(11, 6, 7, sibling)

        @pl.when(slot == 6)
        def _():
            landed_k(7)
            landed_v(7)
            landed_k(10)
            go_k(12, 10, 11, sibling)
            landed_k(12)
            go_k(13, 12, 13, sibling)

        @pl.when(slot == 8)
        def _():
            landed_k(9)
            landed_v(9)
            landed_v(10)
            go_v(12, 10, 11, sibling)
            landed_v(12)
            go_v(13, 12, 13, sibling)
            landed_k(14)
            go_k(14, 14, 15, sibling)
            landed_v(14)
            go_v(14, 14, 15, sibling)

        @pl.when(slot == 10)
        def _():
            landed_k(11)
            landed_v(11)

        @pl.when(slot == 12)
        def _():
            landed_k(13)
            landed_v(13)

        @pl.when(slot == 14)
        def _():
            landed_k(15)
            landed_v(15)

    def owner_step(slot, carry):
        relay(slot)

        def step(j, carry):
            for i in range(SPLITS + 2):
                if i >= 2:
                    score(slot + 1, j, i - 2)
                if 1 <= i <= SPLITS:
                    weigh(i - 1)
                if i < SPLITS:
                    mix(slot, j, i)
            return carry

        return lax.fori_loop(0, TILES, step, carry)

    lax.fori_loop(0, OWNERS - 1, owner_step, 0)
    for i in range(SPLITS + 1):
        if i >= 1:
            weigh(i - 1)
        if i < SPLITS:
            mix(OWNERS - 1, TILES - 2, i)
    for c in range(SPLITS):
        mix(OWNERS - 1, TILES - 1, c)

    per = TILE // NEW
    for h in range(GROUP):
        j, at = h // per, (h % per) * NEW
        part = acc[j, :, at : at + NEW] * (1.0 / den[j, :, at : at + NEW])
        o_ref[:, h * HEAD_DIM : (h + 1) * HEAD_DIM] = part.T.astype(bf16)

    for d in range(1, TP):
        pltpu.make_async_copy(pack.at[0], pack.at[0], p1_send.at[d - 1]).wait()
    for at in range(15):
        gone_n(at)
        gone_k(at)
        gone_v(at)


def on_device(queries, cache_keys, cache_values, new_keys, new_values, sources):
    vmem, dma = pltpu.VMEM, pltpu.SemaphoreType.DMA
    whole = pl.BlockSpec(memory_space=pltpu.VMEM)
    there = pl.BlockSpec(memory_space=pl.ANY)
    return pl.pallas_call(
        kernel,
        out_shape=jax.ShapeDtypeStruct(queries.shape, queries.dtype),
        in_specs=[whole, there, there, whole, whole, whole],
        out_specs=whole,
        scratch_shapes=[
            vmem((OWNERS, CACHE, HEAD_DIM), bf16),
            vmem((OWNERS, HEAD_DIM, CACHE), bf16),
            vmem((OWNERS, 2 * HEAD_DIM, NEW), bf16),
            vmem((OWNERS, NEW, HEAD_DIM), bf16),
            vmem((OWNERS, HEAD_DIM, NEW), bf16),
            vmem((OWNERS, NEW, NEW), f32),
            vmem((OWNERS // 2, OWNERS * NEW, 2 * NEW), bf16),
            vmem((CACHE, HEAD_DIM), bf16),
            vmem((TP, 32, HEAD_DIM), bf16),
            vmem((TP, 32, HEAD_DIM), bf16),
            vmem((ROWS, 2 * HEAD_DIM), bf16),
            vmem((KEYS, TILE), f32),
            vmem((8, TILE), f32),
            vmem((KEYS, TILE), bf16),
            vmem((1, TILE), f32),
            vmem((1, TILE), f32),
            vmem((TILES, HEAD_DIM, TILE), f32),
            vmem((TILES, 1, TILE), f32),
            vmem((TILES, 1, TILE), f32),
            dma((2,)),
            dma((7,)),
            dma((7,)),
            dma((15,)),
            dma((OWNERS,)),
            dma((15,)),
            dma((OWNERS,)),
            dma((15,)),
            dma((OWNERS,)),
        ],
        compiler_params=pltpu.CompilerParams(
            collective_id=0, has_side_effects=True, vmem_limit_bytes=60 * 2**20
        ),
    )(queries, cache_keys, cache_values, new_keys, new_values, sources.reshape(OWNERS, NEW))


def solution(mesh):
    placed = (
        P("ctx", "tp"),
        P("ctx", "tp"),
        P("ctx", "tp"),
        P(("ctx", "tp"), None),
        P(("ctx", "tp"), None),
        P(),
    )
    return jax.shard_map(on_device, mesh=mesh, in_specs=placed, out_specs=P("ctx", "tp"), check_vma=False)
```

```python
import functools
import math

import jax
import jax.numpy as jnp
from jax import lax
from jax.experimental import pallas as pl
from jax.experimental.pallas import tpu as pltpu
from jax.sharding import PartitionSpec as P

HEAD_DIM = 128
GROUP = 16
OWNERS = 16
TP = 8
NEW = 128
CACHE = 1024
KEYS = CACHE + NEW
ROWS = NEW * GROUP
TILE = 1024
TILES = ROWS // TILE
WIDE = 256
SPLITS = TILE // WIDE
AHEAD = 4
MASKED = -1e30
SCALE = math.log2(math.e) / math.sqrt(HEAD_DIM)
MESH = pl.DeviceIdType.MESH
NT = (((1,), (1,)), ((), ()))
f32, bf16 = jnp.float32, jnp.bfloat16

CHIPS = [(0, 0), (-1, 0), (1, 0), (2, 0), (0, 1), (-1, 1), (1, 1), (2, 1)]
GROUP_OF = {chip: i for i, chip in enumerate(CHIPS)}


def kernel(
    q_ref, ck_ref, cv_ref, nk_ref, nv_ref, src_ref, o_ref,
    kc, vc, newk, newv, kn, vn, lim, hot, vtmp, pack, stage, q2, sa, ma, sb, mb, pb, lb, mm, acc, den, top,
    local_sem, p1_send, p1_recv, nk_send, nk_recv, nv_send, nv_recv, k_send, k_recv, v_send, v_recv,
):
    ctx, tp = lax.axis_index("ctx"), lax.axis_index("tp")
    x, yh, core = ctx // 4, (ctx // 2) % 2, ctx % 2

    def owner_at(dx, dy, dc):
        return ((x + dx + 4) % 4) * 4 + ((yh + dy) % 2) * 2 + (core + dc) % 2

    def owner_of(slot):
        group = slot // 2
        place = group % 4
        dx = (3 * place + (place // 2) * (2 * place - 5)) % 4
        return owner_at(dx, group // 4, slot % 2)

    sibling = (owner_at(0, 0, 1), tp)
    right = (owner_at(1, 0, 0), tp)
    left = (owner_at(-1, 0, 0), tp)
    across = (owner_at(0, 1, 0), tp)

    def remote(src, dst, send, recv, to):
        return pltpu.make_async_remote_copy(
            src_ref=src, dst_ref=dst, send_sem=send, recv_sem=recv, device_id=to, device_id_type=MESH
        )

    def carrier(buf, send, recv):
        def go(at, src, dst, to):
            remote(buf.at[src], buf.at[dst], send.at[at], recv.at[dst], to).start()

        def landed(slot):
            pltpu.make_async_copy(buf.at[slot], buf.at[slot], recv.at[slot]).wait()

        def gone(at):
            pltpu.make_async_copy(buf.at[0], buf.at[0], send.at[at]).wait()

        return go, landed, gone

    go_k, landed_k, gone_k = carrier(kc, k_send, k_recv)
    go_v, landed_v, gone_v = carrier(vc, v_send, v_recv)
    go_nk, landed_nk, gone_nk = carrier(newk, nk_send, nk_recv)
    go_nv, landed_nv, gone_nv = carrier(newv, nv_send, nv_recv)

    barrier = pltpu.get_barrier_semaphore()
    peers = [(ctx, (tp + d) % TP) for d in range(1, TP)]
    peers += [(owner_at(dx, dy, 0), tp) for dx, dy in CHIPS[1:]] + [sibling]
    for peer in peers:
        pl.semaphore_signal(barrier, inc=1, device_id=peer, device_id_type=MESH)

    own_k = pltpu.make_async_copy(ck_ref, kc.at[0], local_sem.at[0])
    own_v = pltpu.make_async_copy(cv_ref, vtmp, local_sem.at[1])
    own_k.start()
    own_v.start()
    for h in range(TP):
        cols = slice(h * HEAD_DIM, (h + 1) * HEAD_DIM)
        pack[h, :16, :] = nk_ref[:, cols]
        pack[h, 16:, :] = nv_ref[:, cols]
    stage[tp] = pack[tp]
    own_k.wait()

    pl.semaphore_wait(barrier, len(peers))
    for d in range(1, TP):
        head = (tp + d) % TP
        remote(pack.at[head], stage.at[tp], p1_send.at[d - 1], p1_recv.at[d - 1], (ctx, head)).start()
    go_k(0, 0, 1, sibling)
    go_k(1, 0, 2, right)
    go_k(2, 0, 4, left)

    for h in range(GROUP):
        rows = pl.ds(h * NEW, NEW)
        part = q_ref[:, pl.ds(h * HEAD_DIM, HEAD_DIM)].astype(f32) * SCALE
        high = part.astype(bf16)
        q2[rows, :HEAD_DIM] = high
        q2[rows, HEAD_DIM:] = (part - high.astype(f32)).astype(bf16)
    own_v.wait()
    for b in range(CACHE // 128):
        vc[0, :, b * 128 : (b + 1) * 128] = vtmp[b * 128 : (b + 1) * 128, :].astype(f32).T.astype(bf16)
    go_v(0, 0, 1, sibling)
    acc[...] = jnp.zeros_like(acc)
    den[...] = jnp.zeros_like(den)
    top[...] = jnp.full_like(top, MASKED)

    def limits(slot, carry):
        owner = owner_of(slot)
        pos = jnp.broadcast_to(src_ref[pl.ds(owner, 1), :].astype(f32), (NEW, NEW)).T
        token = (ctx * NEW + lax.broadcasted_iota(jnp.int32, (NEW, NEW), 1)).astype(f32)
        lim[slot] = jnp.where(pos <= token, f32(3e38), f32(MASKED))
        return carry

    lax.fori_loop(0, OWNERS, limits, 0)

    def columns(c):
        return pl.ds(c * WIDE, WIDE)

    def scores(keys, j, c):
        queries = q2[pl.ds(pl.multiple_of(j * TILE + c * WIDE, WIDE), WIDE), :]
        return lax.dot_general(
            jnp.concatenate([keys, keys], axis=1), queries, NT, preferred_element_type=f32
        )

    def peaks(s):
        return jnp.max(s.reshape(s.shape[0] // 8, 8, WIDE), axis=0)

    def masked(s, slot):
        return jnp.minimum(s, jnp.concatenate([lim[slot]] * (WIDE // NEW), axis=1))

    def score(slot, j, c):
        s = scores(jnp.concatenate([kc[slot], kn[slot]], axis=0), j, c)
        cached, new = s[:CACHE], masked(s[CACHE:], slot)
        sb[:CACHE, columns(c)] = cached
        sb[CACHE:, columns(c)] = new
        mb[:, columns(c)] = jnp.maximum(peaks(cached), peaks(new))

    def weigh(c, ahead=None):
        cols = columns(c)
        peak = jnp.max(mb[:, cols], axis=0, keepdims=True)
        total = None
        for at in range(0, KEYS, 128):
            if ahead is None or at >= CACHE:
                s = sb[at : at + 128, cols]
            else:
                s = sa[ahead, at : at + 128, cols]
            w = jnp.exp2(s - peak)
            part = jnp.sum(w.reshape(16, 8, WIDE), axis=0)
            total = part if total is None else total + part
            pb[at : at + 128, cols] = w.astype(bf16)
        lb[:, cols] = jnp.sum(total, axis=0, keepdims=True)
        mm[:, cols] = peak

    def mix(slot, j, c):
        cols = columns(c)
        total, peak = lb[:, cols], mm[:, cols]
        values = jnp.concatenate([vc[slot], vn[slot]], axis=1)
        mixed = jnp.dot(values, pb[:, cols], preferred_element_type=f32)
        partial = (mixed * (1.0 / total)).astype(bf16).astype(f32)
        lse = peak + jnp.log2(total)
        old = top[j, :, cols]
        new = jnp.maximum(old, lse)
        keep, add = jnp.exp2(old - new), jnp.exp2(lse - new)
        acc[j, :, cols] = acc[j, :, cols] * keep + partial * add
        den[j, :, cols] = den[j, :, cols] * keep + add
        top[j, :, cols] = new

    def score_cached(slot, j, ahead):
        for c in range(SPLITS):
            s = scores(kc[slot], j, c)
            sa[ahead, :, columns(c)] = s
            ma[ahead, :, columns(c)] = peaks(s)

    def score_new(slot, j, ahead, c):
        s = masked(scores(kn[slot], j, c), slot)
        sb[CACHE:, columns(c)] = s
        mb[:, columns(c)] = jnp.maximum(ma[ahead, :, columns(c)], peaks(s))

    score_cached(0, 0, 0)

    for d in range(1, TP):
        source = (tp - d + TP) % TP
        pltpu.make_async_copy(stage.at[source], stage.at[source], p1_recv.at[d - 1]).wait()
    for i, (new, go) in enumerate(((newk, go_nk), (newv, go_nv))):
        rows = jnp.concatenate([stage[h, i * 16 : (i + 1) * 16, :] for h in range(TP)], axis=0)
        new[0] = rows.astype(f32).T.astype(bf16)
        for g in (4, 7, 5, 6, 3, 1, 2):
            dx, dy = CHIPS[g]
            back = GROUP_OF[(-dx if abs(dx) == 1 else dx, dy)]
            go(g, 0, 2 * back, (owner_at(dx, dy, 0), tp))
        go(0, 0, 1, sibling)
    go_v(1, 0, 2, right)
    go_v(2, 0, 4, left)
    go_k(3, 0, 8, across)
    score_cached(0, 1, 1)

    def choose(pair, carry):
        want = jnp.concatenate(
            [src_ref[pl.ds(owner_of(2 * pair + i), 1), :] for i in range(2)], axis=1
        )
        for slot in range(OWNERS):
            dx, dy = CHIPS[slot // 2]
            token = owner_at(dx, dy, slot % 2) * NEW + lax.broadcasted_iota(jnp.int32, (NEW, 2 * NEW), 0)
            rows = slice(slot * NEW, (slot + 1) * NEW)
            hot[pair, rows, :] = jnp.where(token == want, f32(1), f32(0)).astype(bf16)
        return carry

    lax.fori_loop(0, OWNERS // 2, choose, 0)

    def pass_over(go, landed):
        for g in (1, 2, 3, 4, 5, 6, 7):
            landed(2 * g)
            go(7 + g, 2 * g, 2 * g + 1, sibling)

    def picked(new, pair):
        rows = jnp.concatenate([new[slot] for slot in range(OWNERS)], axis=1)
        return jnp.dot(rows, hot[pair], preferred_element_type=f32)

    def pick_keys(pair):
        got = picked(newk, pair)
        for i in range(2):
            kn[2 * pair + i] = got[:, i * NEW : (i + 1) * NEW].T.astype(bf16)

    def pick_values(pair):
        got = picked(newv, pair)
        for i in range(2):
            vn[2 * pair + i] = got[:, i * NEW : (i + 1) * NEW].astype(bf16)

    landed_k(1)
    score_cached(1, 0, 2)
    pass_over(go_nk, landed_nk)
    go_v(3, 0, 8, across)
    landed_k(2)
    go_k(4, 2, 6, right)
    go_k(5, 2, 3, sibling)
    landed_k(4)
    go_k(6, 4, 5, sibling)
    score_cached(1, 1, 3)
    for g in range(8):
        landed_nk(2 * g + 1)
    pick_keys(0)
    pass_over(go_nv, landed_nv)
    for c in range(SPLITS):
        score_new(0, 0, 0, c)
    for i in range(SPLITS + 1):
        if i >= 1:
            score_new(0, 1, 1, i - 1)
        if i < SPLITS:
            weigh(i, 0)
    for g in range(8):
        landed_nv(2 * g + 1)
    pick_values(0)

    def relay(slot):
        @pl.when((slot % 2 == 1) & (slot > 1))
        def _():
            pick_keys((slot + 1) // 2)
            pick_values((slot + 1) // 2)

        @pl.when(slot == 2)
        def _():
            landed_k(3)

        @pl.when(slot == 3)
        def _():
            landed_v(3)
            landed_k(6)
            go_k(10, 6, 14, across)
            go_k(11, 6, 7, sibling)
            landed_v(8)
            go_v(7, 8, 10, right)
            go_v(8, 8, 12, left)
            go_v(9, 8, 9, sibling)

        @pl.when(slot == 4)
        def _():
            landed_k(5)
            landed_v(5)
            landed_v(6)
            go_v(10, 6, 14, across)
            go_v(11, 6, 7, sibling)

        @pl.when(slot == 6)
        def _():
            landed_k(7)
            landed_v(7)
            landed_k(10)
            go_k(12, 10, 11, sibling)
            landed_k(12)
            go_k(13, 12, 13, sibling)

        @pl.when(slot == 8)
        def _():
            landed_k(9)
            landed_v(9)
            landed_v(10)
            go_v(12, 10, 11, sibling)
            landed_v(12)
            go_v(13, 12, 13, sibling)
            landed_k(14)
            go_k(14, 14, 15, sibling)
            landed_v(14)
            go_v(14, 14, 15, sibling)

        @pl.when(slot == 10)
        def _():
            landed_k(11)
            landed_v(11)

        @pl.when(slot == 12)
        def _():
            landed_k(13)
            landed_v(13)

        @pl.when(slot == 14)
        def _():
            landed_k(15)
            landed_v(15)

    def light_step(j, carry):
        for i in range(SPLITS + 2):
            if i >= 2:
                score_new(1, j, j + 2, i - 2)
            if 1 <= i <= SPLITS:
                weigh(i - 1, j + 1)
            if i < SPLITS:
                mix(0, j, i)
        return carry

    lax.fori_loop(0, TILES, light_step, 0)
    landed_v(1)
    landed_v(2)
    go_v(4, 2, 3, sibling)
    landed_v(4)
    go_v(5, 4, 6, left)
    go_v(6, 4, 5, sibling)
    landed_k(8)
    go_k(7, 8, 10, right)
    go_k(8, 8, 12, left)
    go_k(9, 8, 9, sibling)
    pick_keys(1)
    pick_values(1)
    for i in range(SPLITS + 2):
        if i >= 2:
            score(2, 0, i - 2)
        if 1 <= i <= SPLITS:
            weigh(i - 1, 3)
        if i < SPLITS:
            mix(1, 0, i)

    def owner_step(slot, carry):
        relay(slot)

        def step(j, carry):
            for i in range(SPLITS + 2):
                if i >= 2:
                    score(slot + 1, j, i - 2)
                if 1 <= i <= SPLITS:
                    weigh(i - 1)
                if i < SPLITS:
                    mix(slot, j, i)
            return carry

        return lax.fori_loop(jnp.maximum(2 - slot, 0), TILES, step, carry)

    lax.fori_loop(1, OWNERS - 1, owner_step, 0)
    for i in range(SPLITS + 1):
        if i >= 1:
            weigh(i - 1)
        if i < SPLITS:
            mix(OWNERS - 1, TILES - 2, i)
    for c in range(SPLITS):
        mix(OWNERS - 1, TILES - 1, c)

    per = TILE // NEW
    for h in range(GROUP):
        j, at = h // per, (h % per) * NEW
        part = acc[j, :, at : at + NEW] * (1.0 / den[j, :, at : at + NEW])
        o_ref[:, h * HEAD_DIM : (h + 1) * HEAD_DIM] = part.T.astype(bf16)

    for d in range(1, TP):
        pltpu.make_async_copy(pack.at[0], pack.at[0], p1_send.at[d - 1]).wait()
    for at in range(15):
        gone_nk(at)
        gone_nv(at)
        gone_k(at)
        gone_v(at)


def on_device(queries, cache_keys, cache_values, new_keys, new_values, sources):
    vmem, dma = pltpu.VMEM, pltpu.SemaphoreType.DMA
    whole = pl.BlockSpec(memory_space=pltpu.VMEM)
    there = pl.BlockSpec(memory_space=pl.ANY)
    return pl.pallas_call(
        kernel,
        out_shape=jax.ShapeDtypeStruct(queries.shape, queries.dtype),
        in_specs=[whole, there, there, whole, whole, whole],
        out_specs=whole,
        scratch_shapes=[
            vmem((OWNERS, CACHE, HEAD_DIM), bf16),
            vmem((OWNERS, HEAD_DIM, CACHE), bf16),
            vmem((OWNERS, HEAD_DIM, NEW), bf16),
            vmem((OWNERS, HEAD_DIM, NEW), bf16),
            vmem((OWNERS, NEW, HEAD_DIM), bf16),
            vmem((OWNERS, HEAD_DIM, NEW), bf16),
            vmem((OWNERS, NEW, NEW), f32),
            vmem((OWNERS // 2, OWNERS * NEW, 2 * NEW), bf16),
            vmem((CACHE, HEAD_DIM), bf16),
            vmem((TP, 32, HEAD_DIM), bf16),
            vmem((TP, 32, HEAD_DIM), bf16),
            vmem((ROWS, 2 * HEAD_DIM), bf16),
            vmem((AHEAD, CACHE, TILE), f32),
            vmem((AHEAD, 8, TILE), f32),
            vmem((KEYS, TILE), f32),
            vmem((8, TILE), f32),
            vmem((KEYS, TILE), bf16),
            vmem((1, TILE), f32),
            vmem((1, TILE), f32),
            vmem((TILES, HEAD_DIM, TILE), f32),
            vmem((TILES, 1, TILE), f32),
            vmem((TILES, 1, TILE), f32),
            dma((2,)),
            dma((7,)),
            dma((7,)),
            dma((15,)),
            dma((OWNERS,)),
            dma((15,)),
            dma((OWNERS,)),
            dma((15,)),
            dma((OWNERS,)),
            dma((15,)),
            dma((OWNERS,)),
        ],
        compiler_params=pltpu.CompilerParams(
            collective_id=0, has_side_effects=True, vmem_limit_bytes=60 * 2**20
        ),
    )(queries, cache_keys, cache_values, new_keys, new_values, sources.reshape(OWNERS, NEW))


def solution(mesh):
    placed = (
        P("ctx", "tp"),
        P("ctx", "tp"),
        P("ctx", "tp"),
        P(("ctx", "tp"), None),
        P(("ctx", "tp"), None),
        P(),
    )
    return jax.shard_map(on_device, mesh=mesh, in_specs=placed, out_specs=P("ctx", "tp"), check_vma=False)
```

```python
import functools
import math

import jax
import jax.numpy as jnp
from jax import lax
from jax.experimental import pallas as pl
from jax.experimental.pallas import tpu as pltpu
from jax.sharding import PartitionSpec as P

HEAD_DIM = 128
GROUP = 16
OWNERS = 16
TP = 8
NEW = 128
CACHE = 1024
KEYS = CACHE + NEW
ROWS = NEW * GROUP
TILE = 1024
TILES = ROWS // TILE
WIDE = 256
SPLITS = TILE // WIDE
AHEAD = 4
MASKED = -1e30
SCALE = math.log2(math.e) / math.sqrt(HEAD_DIM)
MESH = pl.DeviceIdType.MESH
NT = (((1,), (1,)), ((), ()))
f32, bf16 = jnp.float32, jnp.bfloat16

CHIPS = [(0, 0), (-1, 0), (1, 0), (2, 0), (0, 1), (-1, 1), (1, 1), (2, 1)]
GROUP_OF = {chip: i for i, chip in enumerate(CHIPS)}


def kernel(
    q_in, ck_ref, cv_ref, nk_in, nv_in, src_in, o_ref,
    q_ref, nk_ref, nv_ref, src_ref, kc, vc, newk, newv, kn, vn, lim, hot, vtmp, pack, stage, q2, sa, ma, sb, mb, pb, lb, mm, acc, den, top,
    local_sem, p1_send, p1_recv, nk_send, nk_recv, nv_send, nv_recv, k_send, k_recv, v_send, v_recv,
):
    ctx, tp = lax.axis_index("ctx"), lax.axis_index("tp")
    x, yh, core = ctx // 4, (ctx // 2) % 2, ctx % 2

    def owner_at(dx, dy, dc):
        return ((x + dx + 4) % 4) * 4 + ((yh + dy) % 2) * 2 + (core + dc) % 2

    def owner_of(slot):
        group = slot // 2
        place = group % 4
        dx = (3 * place + (place // 2) * (2 * place - 5)) % 4
        return owner_at(dx, group // 4, slot % 2)

    sibling = (owner_at(0, 0, 1), tp)
    right = (owner_at(1, 0, 0), tp)
    left = (owner_at(-1, 0, 0), tp)
    across = (owner_at(0, 1, 0), tp)

    def remote(src, dst, send, recv, to):
        return pltpu.make_async_remote_copy(
            src_ref=src, dst_ref=dst, send_sem=send.at[0], recv_sem=recv, device_id=to, device_id_type=MESH
        )

    def carrier(buf, send, recv):
        def go(at, src, dst, to):
            remote(buf.at[src], buf.at[dst], send, recv.at[dst], to).start()

        def landed(slot):
            pltpu.make_async_copy(buf.at[slot], buf.at[slot], recv.at[slot]).wait()

        def gone():
            every = buf.at[pl.ds(0, 15)]
            pltpu.make_async_copy(every, every, send.at[0]).wait()

        return go, landed, gone

    go_k, landed_k, gone_k = carrier(kc, k_send, k_recv)
    go_v, landed_v, gone_v = carrier(vc, v_send, v_recv)
    go_nk, landed_nk, gone_nk = carrier(newk, nk_send, nk_recv)
    go_nv, landed_nv, gone_nv = carrier(newv, nv_send, nv_recv)

    barrier = pltpu.get_barrier_semaphore()
    peers = [(ctx, (tp + d) % TP) for d in range(1, TP)]
    peers += [(owner_at(dx, dy, 0), tp) for dx, dy in CHIPS[1:]] + [sibling]
    for peer in peers:
        pl.semaphore_signal(barrier, inc=1, device_id=peer, device_id_type=MESH)

    own_k = pltpu.make_async_copy(ck_ref, kc.at[0], local_sem.at[0])
    own_v = pltpu.make_async_copy(cv_ref, vtmp, local_sem.at[1])
    fetched = [
        pltpu.make_async_copy(here, there, local_sem.at[2 + i])
        for i, (here, there) in enumerate(
            ((nk_in, nk_ref), (nv_in, nv_ref), (q_in, q_ref), (src_in, src_ref))
        )
    ]
    for copy in fetched[:2] + [own_k, own_v] + fetched[2:]:
        copy.start()
    for copy in fetched[:2]:
        copy.wait()
    for h in range(TP):
        cols = slice(h * HEAD_DIM, (h + 1) * HEAD_DIM)
        pack[h, :16, :] = nk_ref[:, cols]
        pack[h, 16:, :] = nv_ref[:, cols]
    stage[tp] = pack[tp]
    own_k.wait()

    pl.semaphore_wait(barrier, len(peers))
    for d in range(1, TP):
        head = (tp + d) % TP
        remote(pack.at[head], stage.at[tp], p1_send, p1_recv.at[d - 1], (ctx, head)).start()
    go_k(0, 0, 1, sibling)
    go_k(1, 0, 2, right)
    go_k(2, 0, 4, left)

    for copy in fetched[2:]:
        copy.wait()
    for h in range(GROUP):
        rows = pl.ds(h * NEW, NEW)
        part = q_ref[:, pl.ds(h * HEAD_DIM, HEAD_DIM)].astype(f32) * SCALE
        high = part.astype(bf16)
        q2[rows, :HEAD_DIM] = high
        q2[rows, HEAD_DIM:] = (part - high.astype(f32)).astype(bf16)
    own_v.wait()
    for b in range(CACHE // 128):
        vc[0, :, b * 128 : (b + 1) * 128] = vtmp[b * 128 : (b + 1) * 128, :].astype(f32).T.astype(bf16)
    go_v(0, 0, 1, sibling)
    acc[...] = jnp.zeros_like(acc)
    den[...] = jnp.zeros_like(den)
    top[...] = jnp.full_like(top, MASKED)

    def limits(slot, carry):
        owner = owner_of(slot)
        pos = jnp.broadcast_to(src_ref[pl.ds(owner, 1), :].astype(f32), (NEW, NEW)).T
        token = (ctx * NEW + lax.broadcasted_iota(jnp.int32, (NEW, NEW), 1)).astype(f32)
        lim[slot] = jnp.where(pos <= token, f32(3e38), f32(MASKED))
        return carry

    lax.fori_loop(0, OWNERS, limits, 0)

    def columns(c):
        return pl.ds(c * WIDE, WIDE)

    def scores(keys, j, c):
        queries = q2[pl.ds(pl.multiple_of(j * TILE + c * WIDE, WIDE), WIDE), :]
        return lax.dot_general(
            jnp.concatenate([keys, keys], axis=1), queries, NT, preferred_element_type=f32
        )

    def peaks(s):
        return jnp.max(s.reshape(s.shape[0] // 8, 8, WIDE), axis=0)

    def masked(s, slot):
        return jnp.minimum(s, jnp.concatenate([lim[slot]] * (WIDE // NEW), axis=1))

    def score(slot, j, c):
        s = scores(jnp.concatenate([kc[slot], kn[slot]], axis=0), j, c)
        cached, new = s[:CACHE], masked(s[CACHE:], slot)
        sb[:CACHE, columns(c)] = cached
        sb[CACHE:, columns(c)] = new
        mb[:, columns(c)] = jnp.maximum(peaks(cached), peaks(new))

    def weigh(c, ahead=None):
        cols = columns(c)
        peak = jnp.max(mb[:, cols], axis=0, keepdims=True)
        total = None
        for at in range(0, KEYS, 128):
            if ahead is None or at >= CACHE:
                s = sb[at : at + 128, cols]
            else:
                s = sa[ahead, at : at + 128, cols]
            w = jnp.exp2(s - peak)
            part = jnp.sum(w.reshape(16, 8, WIDE), axis=0)
            total = part if total is None else total + part
            pb[at : at + 128, cols] = w.astype(bf16)
        lb[:, cols] = jnp.sum(total, axis=0, keepdims=True)
        mm[:, cols] = peak

    def mix(slot, j, c):
        cols = columns(c)
        total, peak = lb[:, cols], mm[:, cols]
        values = jnp.concatenate([vc[slot], vn[slot]], axis=1)
        mixed = jnp.dot(values, pb[:, cols], preferred_element_type=f32)
        partial = (mixed * (1.0 / total)).astype(bf16).astype(f32)
        lse = peak + jnp.log2(total)
        old = top[j, :, cols]
        new = jnp.maximum(old, lse)
        keep, add = jnp.exp2(old - new), jnp.exp2(lse - new)
        acc[j, :, cols] = acc[j, :, cols] * keep + partial * add
        den[j, :, cols] = den[j, :, cols] * keep + add
        top[j, :, cols] = new

    def score_cached(slot, j, ahead):
        for c in range(SPLITS):
            s = scores(kc[slot], j, c)
            sa[ahead, :, columns(c)] = s
            ma[ahead, :, columns(c)] = peaks(s)

    def score_new(slot, j, ahead, c):
        s = masked(scores(kn[slot], j, c), slot)
        sb[CACHE:, columns(c)] = s
        mb[:, columns(c)] = jnp.maximum(ma[ahead, :, columns(c)], peaks(s))

    score_cached(0, 0, 0)

    for d in range(1, TP):
        source = (tp - d + TP) % TP
        pltpu.make_async_copy(stage.at[source], stage.at[source], p1_recv.at[d - 1]).wait()
    for i, (new, go) in enumerate(((newk, go_nk), (newv, go_nv))):
        rows = jnp.concatenate([stage[h, i * 16 : (i + 1) * 16, :] for h in range(TP)], axis=0)
        new[0] = rows.astype(f32).T.astype(bf16)
        for g in (4, 7, 5, 6, 3, 1, 2):
            dx, dy = CHIPS[g]
            back = GROUP_OF[(-dx if abs(dx) == 1 else dx, dy)]
            go(g, 0, 2 * back, (owner_at(dx, dy, 0), tp))
        go(0, 0, 1, sibling)
    go_v(1, 0, 2, right)
    go_v(2, 0, 4, left)
    go_k(3, 0, 8, across)
    score_cached(0, 1, 1)

    def choose(pair, carry):
        want = jnp.concatenate(
            [src_ref[pl.ds(owner_of(2 * pair + i), 1), :] for i in range(2)], axis=1
        )
        for slot in range(OWNERS):
            dx, dy = CHIPS[slot // 2]
            token = owner_at(dx, dy, slot % 2) * NEW + lax.broadcasted_iota(jnp.int32, (NEW, 2 * NEW), 0)
            rows = slice(slot * NEW, (slot + 1) * NEW)
            hot[pair, rows, :] = jnp.where(token == want, f32(1), f32(0)).astype(bf16)
        return carry

    lax.fori_loop(0, OWNERS // 2, choose, 0)

    def pass_over(go, landed):
        for g in (1, 2, 3, 4, 5, 6, 7):
            landed(2 * g)
            go(7 + g, 2 * g, 2 * g + 1, sibling)

    def everyone(new):
        return jnp.concatenate([new[slot] for slot in range(OWNERS)], axis=1)

    def picked(rows, pair):
        return jnp.dot(rows, hot[pair], preferred_element_type=f32)

    def pick_keys(pair):
        got = picked(everyone(newk), pair)
        for i in range(2):
            kn[2 * pair + i] = got[:, i * NEW : (i + 1) * NEW].T.astype(bf16)

    def pick_values(pair):
        got = picked(everyone(newv), pair)
        for i in range(2):
            vn[2 * pair + i] = got[:, i * NEW : (i + 1) * NEW].astype(bf16)

    def pick(pair):
        got = picked(jnp.concatenate([everyone(newk), everyone(newv)], axis=0), pair)
        for i in range(2):
            kn[2 * pair + i] = got[:HEAD_DIM, i * NEW : (i + 1) * NEW].T.astype(bf16)
            vn[2 * pair + i] = got[HEAD_DIM:, i * NEW : (i + 1) * NEW].astype(bf16)

    landed_k(1)
    score_cached(1, 0, 2)
    pass_over(go_nk, landed_nk)
    go_v(3, 0, 8, across)
    landed_k(2)
    go_k(4, 2, 6, right)
    go_k(5, 2, 3, sibling)
    landed_k(4)
    go_k(6, 4, 5, sibling)
    score_cached(1, 1, 3)
    for g in range(8):
        landed_nk(2 * g + 1)
    pick_keys(0)
    pass_over(go_nv, landed_nv)
    for c in range(SPLITS):
        score_new(0, 0, 0, c)
    for i in range(SPLITS + 1):
        if i >= 1:
            score_new(0, 1, 1, i - 1)
        if i < SPLITS:
            weigh(i, 0)
    for g in range(8):
        landed_nv(2 * g + 1)
    pick_values(0)

    def relay(slot):
        @pl.when((slot % 2 == 1) & (slot > 1))
        def _():
            pick((slot + 1) // 2)

        @pl.when(slot == 2)
        def _():
            landed_k(3)

        @pl.when(slot == 3)
        def _():
            landed_v(3)
            landed_v(8)
            go_v(7, 8, 10, right)
            go_v(8, 8, 12, left)
            go_v(9, 8, 9, sibling)

        @pl.when(slot == 4)
        def _():
            landed_k(5)
            landed_v(5)
            landed_k(6)
            go_k(10, 6, 14, across)
            go_k(11, 6, 7, sibling)

        @pl.when(slot == 6)
        def _():
            landed_k(7)
            landed_v(6)
            go_v(10, 6, 14, across)
            go_v(11, 6, 7, sibling)

        @pl.when(slot == 7)
        def _():
            landed_v(7)
            landed_k(10)
            go_k(12, 10, 11, sibling)
            landed_k(12)
            go_k(13, 12, 13, sibling)

        @pl.when(slot == 8)
        def _():
            landed_k(9)
            landed_v(9)

        @pl.when(slot == 9)
        def _():
            landed_v(10)
            go_v(12, 10, 11, sibling)
            landed_v(12)
            go_v(13, 12, 13, sibling)

        @pl.when(slot == 10)
        def _():
            landed_k(11)
            landed_k(14)
            go_k(14, 14, 15, sibling)
            landed_v(14)
            go_v(14, 14, 15, sibling)

        @pl.when(slot == 11)
        def _():
            landed_v(11)

        @pl.when(slot == 12)
        def _():
            landed_k(13)
            landed_v(13)

        @pl.when(slot == 14)
        def _():
            landed_k(15)
            landed_v(15)

    def light_step(j, carry):
        for i in range(SPLITS + 2):
            if i >= 2:
                score_new(1, j, j + 2, i - 2)
            if 1 <= i <= SPLITS:
                weigh(i - 1, j + 1)
            if i < SPLITS:
                mix(0, j, i)
        return carry

    lax.fori_loop(0, TILES, light_step, 0)
    landed_v(1)
    landed_v(2)
    go_v(4, 2, 3, sibling)
    landed_v(4)
    go_v(5, 4, 6, left)
    go_v(6, 4, 5, sibling)
    landed_k(8)
    go_k(7, 8, 10, right)
    go_k(8, 8, 12, left)
    go_k(9, 8, 9, sibling)
    pick(1)
    for i in range(SPLITS + 2):
        if i >= 2:
            score(2, 0, i - 2)
        if 1 <= i <= SPLITS:
            weigh(i - 1, 3)
        if i < SPLITS:
            mix(1, 0, i)

    def owner_step(slot, carry):
        relay(slot)

        def step(j, carry):
            for i in range(SPLITS + 2):
                if i >= 2:
                    score(slot + 1, j, i - 2)
                if 1 <= i <= SPLITS:
                    weigh(i - 1)
                if i < SPLITS:
                    mix(slot, j, i)
            return carry

        return lax.fori_loop(jnp.maximum(2 - slot, 0), TILES, step, carry)

    lax.fori_loop(1, OWNERS - 1, owner_step, 0)
    for i in range(SPLITS + 1):
        if i >= 1:
            weigh(i - 1)
        if i < SPLITS:
            mix(OWNERS - 1, TILES - 2, i)
    for c in range(SPLITS):
        mix(OWNERS - 1, TILES - 1, c)

    per = TILE // NEW
    for h in range(GROUP):
        j, at = h // per, (h % per) * NEW
        part = acc[j, :, at : at + NEW] * (1.0 / den[j, :, at : at + NEW])
        o_ref[:, h * HEAD_DIM : (h + 1) * HEAD_DIM] = part.T.astype(bf16)

    packs = pack.at[pl.ds(0, TP - 1)]
    pltpu.make_async_copy(packs, packs, p1_send.at[0]).wait()
    gone_nk()
    gone_nv()
    gone_k()
    gone_v()


def on_device(queries, cache_keys, cache_values, new_keys, new_values, sources):
    vmem, dma = pltpu.VMEM, pltpu.SemaphoreType.DMA
    whole = pl.BlockSpec(memory_space=pltpu.VMEM)
    there = pl.BlockSpec(memory_space=pl.ANY)
    return pl.pallas_call(
        kernel,
        out_shape=jax.ShapeDtypeStruct(queries.shape, queries.dtype),
        in_specs=[there] * 6,
        out_specs=whole,
        scratch_shapes=[
            vmem(queries.shape, bf16),
            vmem(new_keys.shape, bf16),
            vmem(new_values.shape, bf16),
            vmem((OWNERS, NEW), jnp.int32),
            vmem((OWNERS, CACHE, HEAD_DIM), bf16),
            vmem((OWNERS, HEAD_DIM, CACHE), bf16),
            vmem((OWNERS, HEAD_DIM, NEW), bf16),
            vmem((OWNERS, HEAD_DIM, NEW), bf16),
            vmem((OWNERS, NEW, HEAD_DIM), bf16),
            vmem((OWNERS, HEAD_DIM, NEW), bf16),
            vmem((OWNERS, NEW, NEW), f32),
            vmem((OWNERS // 2, OWNERS * NEW, 2 * NEW), bf16),
            vmem((CACHE, HEAD_DIM), bf16),
            vmem((TP, 32, HEAD_DIM), bf16),
            vmem((TP, 32, HEAD_DIM), bf16),
            vmem((ROWS, 2 * HEAD_DIM), bf16),
            vmem((AHEAD, CACHE, TILE), f32),
            vmem((AHEAD, 8, TILE), f32),
            vmem((KEYS, TILE), f32),
            vmem((8, TILE), f32),
            vmem((KEYS, TILE), bf16),
            vmem((1, TILE), f32),
            vmem((1, TILE), f32),
            vmem((TILES, HEAD_DIM, TILE), f32),
            vmem((TILES, 1, TILE), f32),
            vmem((TILES, 1, TILE), f32),
            dma((6,)),
            dma((1,)),
            dma((7,)),
            dma((1,)),
            dma((OWNERS,)),
            dma((1,)),
            dma((OWNERS,)),
            dma((1,)),
            dma((OWNERS,)),
            dma((1,)),
            dma((OWNERS,)),
        ],
        compiler_params=pltpu.CompilerParams(
            collective_id=0, has_side_effects=True, vmem_limit_bytes=60 * 2**20
        ),
    )(queries, cache_keys, cache_values, new_keys, new_values, sources.reshape(OWNERS, NEW))


def solution(mesh):
    placed = (
        P("ctx", "tp"),
        P("ctx", "tp"),
        P("ctx", "tp"),
        P(("ctx", "tp"), None),
        P(("ctx", "tp"), None),
        P(),
    )
    return jax.shard_map(on_device, mesh=mesh, in_specs=placed, out_specs=P("ctx", "tp"), check_vma=False)
```
